32 devices in a mesh: blk: 16 (over z, x, core), tp: 2 (over y).
Axes of the slice: x: 2, y: 2, z: 4, core: 2. Of those that a mesh axis runs over, the one named last changes fastest.
Arguments:
- hidden_in: bfloat16 [6144, 4096], P('blk'), may hold values from -6 to 6
- w_query: bfloat16 [4096, 4096], P('blk', 'tp'), may hold values from -0.09375 to 0.09375
- w_key: bfloat16 [4096, 1024], P('blk', 'tp'), may hold values from -0.09375 to 0.09375
- w_value: bfloat16 [4096, 1024], P('blk', 'tp'), may hold values from -0.09375 to 0.09375
- starts: int32 [16], P('blk'), may hold values from 0 to 1152, as said below
- key_cache: bfloat16 [16, 1152, 1024], P('blk', None, 'tp'), may hold values from -400 to 400
- value_cache: bfloat16 [16, 1152, 1024], P('blk', None, 'tp'), may hold values from -6 to 6
- grad_out: bfloat16 [6144, 4096], P('blk', 'tp'), may hold values from -6 to 6
Outputs:
- attended: bfloat16 [6144, 4096], P('blk', 'tp')
- grad_in: bfloat16 [6144, 4096], P('blk', 'tp')
- grad_wq: float32 [4096, 4096], P('blk', 'tp')
- grad_wk: float32 [4096, 1024], P('blk', 'tp')
- grad_wv: float32 [4096, 1024], P('blk', 'tp')
The draws below stay inside these ranges and needn't reach their ends.
Inputs may be any that keep to these rules, and one draw needn't show every extreme that they name: `starts`: every entry is a multiple of 384; both 0 and 1152 occur.
All inputs are finite; a program needn't handle non-finite values.
Results may differ from the reference program's by a relative error of at most 0.025.
The reference program's roundings to bfloat16 on the way count: a program that leaves them out, or rounds other values in their place, can miss the bound.
Values may be sent and summed in bfloat16 or wider, within the bound.
A program may use at most 128 MiB of HBM per device.

```python
import jax
import jax.numpy as jnp
from jax import lax

D = 4096
H = 32
KV = 8
HD = 128
TOK_DEV = 384
CACHE_BLOCKS = 3
CACHE = 1152
TOKENS = 6144
N_BLK = 16


def draw_starts(key, part):
    order = jax.random.permutation(key, N_BLK)
    return (order % (CACHE_BLOCKS + 1) * TOK_DEV).astype(jnp.int32)


def draw_key_cache(key, part):
    base = jnp.clip(jax.random.normal(key, (N_BLK, CACHE, KV * HD), jnp.float32), -4.0, 4.0)
    return base.astype(jnp.bfloat16)


def with_spikes(result, key, source, target, shards_of, factor):
    owner, partner = [(jnp.arange(result.shape[dim]) // (result.shape[dim] // shards_of)).reshape([-1 if axis == dim else 1 for axis in range(result.ndim)]) for dim in (source, target)]
    chosen = jax.random.permutation(key, shards_of)[partner]
    strong = (owner == chosen) | (owner == (partner + shards_of // 2) % shards_of)
    return jnp.where(strong, factor * result, result)


def block_scale(own_key, extent, cuts, least, high):
    loudness, own = 1.0, jax.random.fold_in(own_key, 6)
    for position, blocks in cuts:
        steps = jnp.exp(jax.random.uniform(jax.random.fold_in(own, position), (blocks,), jnp.float32, least / len(cuts), high / len(cuts)))
        loudness = loudness * jnp.repeat(steps, extent[position] // blocks).reshape([-1 if axis == position else 1 for axis in range(len(extent))])
    return loudness


def centred(rng, extent, deviation, limit, split=(), held_as=jnp.bfloat16):
    gain = block_scale(rng, extent, split, -0.22, 0.18) if split else 1.0
    result = jax.random.normal(rng, extent, jnp.float32) * deviation * gain
    return jnp.minimum(jnp.maximum(result, -limit), limit).astype(held_as)


def gaussian_with(own_key, shape, deviation, reach, cuts, heavy, kind=jnp.bfloat16):
    entries = deviation * jax.random.normal(own_key, shape, jnp.float32)
    if cuts:
        entries = entries * block_scale(own_key, shape, cuts, -0.22, 0.18)
    return jnp.clip(with_spikes(entries, jax.random.fold_in(own_key, 3), *heavy), -reach, reach).astype(kind)


def setup_inputs(seed: int = 0) -> dict:
    key_of = jax.random.split(jax.random.key(seed), 9)
    hidden_in = gaussian_with(key_of[0], (TOKENS, D), 1.0, 6.0, ((0, 16),), (0, 1, 16, 2.0))
    w_query = centred(key_of[1], (D, H * HD), D ** -0.5, 0.09375, ((0, 16), (1, 2)))
    w_key = centred(key_of[2], (D, KV * HD), D ** -0.5, 0.09375, ((0, 16), (1, 2)))
    w_value = centred(key_of[3], (D, KV * HD), D ** -0.5, 0.09375, ((0, 16), (1, 2)))
    starts = draw_starts(jax.random.fold_in(key_of[8], 71), 0)
    key_cache = draw_key_cache(jax.random.fold_in(key_of[8], 71), 0)
    value_cache = centred(key_of[6], (N_BLK, CACHE, KV * HD), 1.0, 6.0, ((0, 16), (2, 2)))
    grad_out = centred(key_of[7], (TOKENS, H * HD), 1.0, 6.0, ((0, 16), (1, 2)))
    return {"hidden_in": hidden_in, "w_query": w_query, "w_key": w_key, "w_value": w_value, "starts": starts, "key_cache": key_cache, "value_cache": value_cache, "grad_out": grad_out}


def contract_last(left, right):
    return lax.dot_general(left, right, (((1,), (1,)), ((), ())), preferred_element_type=jnp.float32)


def contract_first(left, right):
    return lax.dot_general(left, right, (((0,), (0,)), ((), ())), preferred_element_type=jnp.float32)


def head_pass(queries, cache_keys, cache_values, fresh_keys, fresh_values, grad_heads, offset):
    groups, row_count, head_width = queries.shape
    cached = cache_keys.shape[0]
    factor = head_width ** -0.5
    key_list = jnp.concatenate([cache_keys, fresh_keys], 0)
    value_list = jnp.concatenate([cache_values, fresh_values], 0)
    flat_query = queries.reshape(groups * row_count, head_width)
    flat_grad = grad_heads.reshape(groups * row_count, head_width)
    scores = contract_last(flat_query, key_list) * factor
    scores = scores.reshape(groups, row_count, cached + row_count)
    row_pos = lax.iota(jnp.int32, row_count)
    cache_ok = jnp.broadcast_to(lax.iota(jnp.int32, cached)[None, :] < offset, (row_count, cached))
    own_ok = row_pos[None, :] <= row_pos[:, None]
    allowed = jnp.concatenate([cache_ok, own_ok], 1)
    scores = jnp.where(allowed[None], scores, -jnp.inf)
    row_max = jnp.max(scores, axis=-1, keepdims=True)
    expo = jnp.exp(scores - row_max)
    probs = (expo / jnp.sum(expo, axis=-1, keepdims=True)).astype(jnp.bfloat16)
    probs = probs.reshape(groups * row_count, cached + row_count)
    attended = jnp.dot(probs, value_list, preferred_element_type=jnp.float32).astype(jnp.bfloat16)
    grad_probs = contract_last(flat_grad, value_list)
    probs_wide = probs.astype(jnp.float32)
    row_dot = jnp.sum(probs_wide * grad_probs, axis=-1, keepdims=True)
    grad_scores = (probs_wide * (grad_probs - row_dot) * factor).astype(jnp.bfloat16)
    grad_query = jnp.dot(grad_scores, key_list, preferred_element_type=jnp.float32).astype(jnp.bfloat16)
    grad_keys = contract_first(grad_scores[:, cached:], flat_query).astype(jnp.bfloat16)
    grad_values = contract_first(probs[:, cached:], flat_grad).astype(jnp.bfloat16)
    return (attended.reshape(groups, row_count, head_width), grad_query.reshape(groups, row_count, head_width), grad_keys, grad_values)


def reference(hidden_in, w_query, w_key, w_value, starts, key_cache, value_cache, grad_out):
    group = H // KV
    queries = jnp.dot(hidden_in, w_query, preferred_element_type=jnp.float32).astype(jnp.bfloat16)
    new_keys = jnp.dot(hidden_in, w_key, preferred_element_type=jnp.float32).astype(jnp.bfloat16)
    new_values = jnp.dot(hidden_in, w_value, preferred_element_type=jnp.float32).astype(jnp.bfloat16)
    per_query = queries.reshape(N_BLK, TOK_DEV, KV, group, HD).transpose(0, 2, 3, 1, 4)
    per_grad = grad_out.reshape(N_BLK, TOK_DEV, KV, group, HD).transpose(0, 2, 3, 1, 4)
    cache_k = key_cache.reshape(N_BLK, CACHE, KV, HD).transpose(0, 2, 1, 3)
    cache_v = value_cache.reshape(N_BLK, CACHE, KV, HD).transpose(0, 2, 1, 3)
    fresh_k = new_keys.reshape(N_BLK, TOK_DEV, KV, HD).transpose(0, 2, 1, 3)
    fresh_v = new_values.reshape(N_BLK, TOK_DEV, KV, HD).transpose(0, 2, 1, 3)

    def per_block(packed):
        offset = packed[6]
        return lax.map(lambda inner: head_pass(*inner, offset), packed[:6])

    results = lax.map(per_block, (per_query, cache_k, cache_v, fresh_k, fresh_v, per_grad, starts))
    attended = results[0].transpose(0, 3, 1, 2, 4).reshape(TOKENS, H * HD)
    grad_query = results[1].transpose(0, 3, 1, 2, 4).reshape(TOKENS, H * HD)
    grad_keys = results[2].transpose(0, 2, 1, 3).reshape(TOKENS, KV * HD)
    grad_values = results[3].transpose(0, 2, 1, 3).reshape(TOKENS, KV * HD)
    grad_in = (contract_last(grad_query, w_query) + contract_last(grad_keys, w_key) + contract_last(grad_values, w_value)).astype(jnp.bfloat16)
    factor = TOKENS ** -0.5
    grad_wq = contract_first(hidden_in, grad_query) * factor
    grad_wk = contract_first(hidden_in, grad_keys) * factor
    grad_wv = contract_first(hidden_in, grad_values) * factor
    return (attended, grad_in, grad_wq, grad_wk, grad_wv)
```

```python
import functools

import jax
import jax.numpy as jnp
from jax import lax
from jax.experimental import pallas as pl
from jax.experimental.pallas import tpu as pltpu
from jax.sharding import PartitionSpec as P

H = 32
KV = 8
HD = 128
MESH = pl.DeviceIdType.MESH
LOG2E = 1.4426950408889634
VMEM_LIMIT = 60 * 1024 * 1024


def contract_last(left, right):
    return lax.dot_general(
        left, right, (((1,), (1,)), ((), ())), preferred_element_type=jnp.float32
    )


def contract_first(left, right):
    return lax.dot_general(
        left, right, (((0,), (0,)), ((), ())), preferred_element_type=jnp.float32
    )


def ring_position(chip, n):
    half = n // 2
    if n == 8:
        z, x = chip // 2, chip % 2
    else:
        z, x = chip % half, chip // half
    return z + x * (n - 1 - 2 * z)


def ring_chip(position, n):
    half = n // 2
    x = position // half
    z = position + x * (n - 1 - 2 * position)
    return z * 2 + x if n == 8 else x * half + z


def places(n):
    blk = lax.axis_index("blk")
    core, chip = blk % 2, blk // 2
    position = ring_position(chip, n)

    def device(pos):
        return ring_chip((pos + 2 * n) % n, n) * 2 + core

    return blk, chip * 2 + 1 - core, position, device


def gather_kernel(
    n, w_ref, hidden_ref, full_ref, pair_ref,
    own_sem, own_send, own_recv, hid_send, hid_recv, ring_send, ring_recv, fwd_send, fwd_recv,
):
    blk, sibling, position, device = places(n)
    target = (device(position + 1), device(position - 1))
    quarter = w_ref.shape[0] // 4
    barrier = pltpu.get_barrier_semaphore()
    for other in (sibling,) + target:
        pl.semaphore_signal(barrier, inc=1, device_id={"blk": other}, device_id_type=MESH)
    pl.semaphore_wait(barrier, 3)

    def origin(way, step):
        return device(position - step) if way == 0 else device(position + step)

    def rows(way, k):
        return pl.ds((way * 2 + k) * quarter, quarter)

    def ring_copy(way, k, step, src, index):
        return pltpu.make_async_remote_copy(
            src_ref=src,
            dst_ref=full_ref.at[index, rows(way, k)],
            send_sem=ring_send.at[way, k, step],
            recv_sem=ring_recv.at[way, k, step],
            device_id={"blk": target[way]},
            device_id_type=MESH,
        )

    def forward(way, k, step, index):
        return pltpu.make_async_remote_copy(
            src_ref=full_ref.at[index, rows(way, k)],
            dst_ref=full_ref.at[index, rows(way, k)],
            send_sem=fwd_send.at[way, k, step],
            recv_sem=fwd_recv.at[way, k, step],
            device_id={"blk": sibling},
            device_id_type=MESH,
        )

    for k in range(2):
        for way in range(2):
            ring_copy(way, k, 0, w_ref.at[rows(way, k)], blk).start()
    own = pltpu.make_async_copy(w_ref, full_ref.at[blk], own_sem)
    own.start()
    share = pltpu.make_async_remote_copy(
        src_ref=w_ref, dst_ref=full_ref.at[blk], send_sem=own_send, recv_sem=own_recv,
        device_id={"blk": sibling}, device_id_type=MESH,
    )
    share.start()
    share_hidden = pltpu.make_async_remote_copy(
        src_ref=hidden_ref, dst_ref=pair_ref, send_sem=hid_send, recv_sem=hid_recv,
        device_id={"blk": sibling}, device_id_type=MESH,
    )
    share_hidden.start()

    def step_body(step, carry):
        for k in range(2):
            for way in range(2):
                index = origin(way, step)
                here = full_ref.at[index, rows(way, k)]
                ring_copy(way, k, step - 1, here, index).wait_recv()

                @pl.when(step < n - 1)
                def _():
                    ring_copy(way, k, step, here, index).start()

                forward(way, k, step - 1, index).start()
        return carry

    lax.fori_loop(1, n, step_body, 0)

    def drain(step, carry):
        for k in range(2):
            for way in range(2):
                index = origin(way, step)
                here = full_ref.at[index, rows(way, k)]
                ring_copy(way, k, step, here, index).wait_send()
                far = origin(way, step + 1)
                mate = far + sibling - blk
                forward(way, k, step, far).wait_send()
                forward(way, k, step, mate).wait_recv()
        return carry

    lax.fori_loop(0, n - 1, drain, 0)
    own.wait()
    share.wait_send()
    pltpu.make_async_remote_copy(
        src_ref=w_ref, dst_ref=full_ref.at[sibling], send_sem=own_send, recv_sem=own_recv,
        device_id={"blk": sibling}, device_id_type=MESH,
    ).wait_recv()
    share_hidden.wait()


def gather(w, hidden, blk_count):
    n = blk_count // 2
    rows, cols = w.shape
    dma = pltpu.SemaphoreType.DMA
    return pl.pallas_call(
        functools.partial(gather_kernel, n),
        out_shape=(
            jax.ShapeDtypeStruct((blk_count, rows, cols), w.dtype),
            jax.ShapeDtypeStruct(hidden.shape, hidden.dtype),
        ),
        in_specs=[pl.BlockSpec(memory_space=pl.ANY)] * 2,
        out_specs=[pl.BlockSpec(memory_space=pl.ANY)] * 2,
        scratch_shapes=[dma, dma, dma, dma, dma] + [dma((2, 2, n - 1))] * 4,
        compiler_params=pltpu.CompilerParams(collective_id=0, has_side_effects=True),
        name="ring_gather",
    )(w, hidden)


def scatter_kernel(
    n, tp_count, scale, hid_ref, mate_ref, grads_ref, term_ref, out_ref, recv_term_ref,
    mate_grads, part, send_buf, recv_buf,
    gr_send, gr_recv, term_send, term_recv, ring_send, ring_recv,
):
    blk, sibling, position, device = places(n)
    target = (device(position + 1), device(position - 1))
    tp_me = lax.axis_index("tp")
    height, width = out_ref.shape
    half_rows, half = height // 2, width // 2
    tile = 384 if half % 384 == 0 else 128
    chunk = term_ref.shape[1] // tp_count
    barrier = pltpu.get_barrier_semaphore()
    for other in (sibling,) + target:
        pl.semaphore_signal(barrier, inc=1, device_id={"blk": other}, device_id_type=MESH)
    for k in range(1, tp_count):
        pl.semaphore_signal(
            barrier, inc=1, device_id={"tp": (tp_me + k) % tp_count}, device_id_type=MESH
        )
    pl.semaphore_wait(barrier, 3 + tp_count - 1)

    share = pltpu.make_async_remote_copy(
        src_ref=grads_ref, dst_ref=mate_grads, send_sem=gr_send, recv_sem=gr_recv,
        device_id={"blk": sibling}, device_id_type=MESH,
    )
    share.start()
    terms = []
    for k in range(1, tp_count):
        peer = (tp_me + k) % tp_count
        copy = pltpu.make_async_remote_copy(
            src_ref=term_ref.at[:, pl.ds(pl.multiple_of(peer * chunk, 128), chunk)],
            dst_ref=recv_term_ref.at[k - 1],
            send_sem=term_send.at[k - 1],
            recv_sem=term_recv.at[k - 1],
            device_id={"tp": peer},
            device_id_type=MESH,
        )
        copy.start()
        terms.append(copy)
    share.wait()

    def ring_copy(way, k, step):
        spot = pl.ds(k * half_rows, half_rows)
        return pltpu.make_async_remote_copy(
            src_ref=send_buf.at[way, step, spot],
            dst_ref=recv_buf.at[way, step, spot],
            send_sem=ring_send.at[way, k, step],
            recv_sem=ring_recv.at[way, k, step],
            device_id={"blk": target[way]},
            device_id_type=MESH,
        )

    def step_body(step, carry):
        for way in range(2):
            owner = device(position - 1 - step) if way == 0 else device(position + 1 + step)
            columns = pl.ds(pl.multiple_of(owner * height, 128), height)

            def tile_body(t, inner):
                at = pl.multiple_of(way * half + t * tile, 128)
                to = pl.multiple_of(t * tile, 128)
                part[way, :, pl.ds(to, tile)] = contract_first(
                    hid_ref[:, columns], grads_ref[:, pl.ds(at, tile)]
                ) + contract_first(mate_ref[:, columns], mate_grads[:, pl.ds(at, tile)])
                return inner

            lax.fori_loop(0, half // tile, tile_body, 0)
        for k in range(2):
            for way in range(2):
                spot = pl.ds(k * half_rows, half_rows)

                @pl.when(step > 0)
                def _():
                    before = step - 1
                    ring_copy(way, k, before).wait_recv()
                    part[way, spot] += recv_buf[way, before, spot].astype(jnp.float32)

                @pl.when(step < n - 1)
                def _():
                    send_buf[way, step, spot] = part[way, spot].astype(jnp.bfloat16)
                    ring_copy(way, k, step).start()

        return carry

    lax.fori_loop(0, n, step_body, 0)
    for way in range(2):
        out_ref[:, way * half : (way + 1) * half] = part[way] * scale

    def drain(step, carry):
        for k in range(2):
            for way in range(2):
                ring_copy(way, k, step).wait_send()
        return carry

    lax.fori_loop(0, n - 1, drain, 0)
    for copy in terms:
        copy.wait()


def scatter(hidden, mate, grads, term, blk_count, tp_count, scale):
    n = blk_count // 2
    tokens, depth = hidden.shape
    height, width = depth // blk_count, grads.shape[1]
    half = width // 2
    dma = pltpu.SemaphoreType.DMA
    vmem = pl.BlockSpec(memory_space=pltpu.VMEM)
    hbm = pl.BlockSpec(memory_space=pl.ANY)
    return pl.pallas_call(
        functools.partial(scatter_kernel, n, tp_count, scale),
        out_shape=(
            jax.ShapeDtypeStruct((height, width), jnp.float32),
            jax.ShapeDtypeStruct((tp_count - 1, tokens, depth // tp_count), jnp.bfloat16),
        ),
        in_specs=[vmem, vmem, vmem, hbm],
        out_specs=[vmem, hbm],
        scratch_shapes=[
            pltpu.VMEM((tokens, width), jnp.bfloat16),
            pltpu.VMEM((2, height, half), jnp.float32),
            pltpu.VMEM((2, n - 1, height, half), jnp.bfloat16),
            pltpu.VMEM((2, n - 1, height, half), jnp.bfloat16),
            dma,
            dma,
            dma((tp_count - 1,)),
            dma((tp_count - 1,)),
            dma((2, 2, n - 1)),
            dma((2, 2, n - 1)),
        ],
        compiler_params=pltpu.CompilerParams(
            collective_id=1, has_side_effects=True, vmem_limit_bytes=VMEM_LIMIT
        ),
        name="ring_scatter",
    )(hidden, mate, grads, term)


def attention_kernel(
    starts_ref, q_ref, kn_ref, vn_ref, kc_ref, vc_ref, go_ref,
    att_ref, gq_ref, gk_ref, gv_ref, gk_acc, gv_acc,
):
    member, group = pl.program_id(1), pl.num_programs(1)
    rows, cached = q_ref.shape[0], kc_ref.shape[1]
    factor = HD ** (-0.5)
    q, go = q_ref[...], go_ref[...]
    kn, vn, kc, vc = kn_ref[...], vn_ref[...], kc_ref[0], vc_ref[0]
    slot = lax.broadcasted_iota(jnp.int32, (rows, cached), 1)
    s_c = jnp.where(slot < starts_ref[0], contract_last(q, kc), -jnp.inf)
    row = lax.broadcasted_iota(jnp.int32, (rows, rows), 0)
    col = lax.broadcasted_iota(jnp.int32, (rows, rows), 1)
    s_o = jnp.where(col <= row, contract_last(q, kn), -jnp.inf)
    top = jnp.maximum(
        jnp.max(s_c, axis=-1, keepdims=True), jnp.max(s_o, axis=-1, keepdims=True)
    )
    e_c = jnp.exp2((s_c - top) * (factor * LOG2E))
    e_o = jnp.exp2((s_o - top) * (factor * LOG2E))
    total = jnp.sum(e_c, axis=-1, keepdims=True) + jnp.sum(e_o, axis=-1, keepdims=True)
    inverse = 1.0 / total
    p_c = (e_c * inverse).astype(jnp.bfloat16)
    p_o = (e_o * inverse).astype(jnp.bfloat16)
    att = jnp.dot(p_c, vc, preferred_element_type=jnp.float32) + jnp.dot(
        p_o, vn, preferred_element_type=jnp.float32
    )
    att_ref[...] = att.astype(jnp.bfloat16)
    row_dot = jnp.sum(att * go.astype(jnp.float32), axis=-1, keepdims=True)
    g_c = contract_last(go, vc) - row_dot
    g_o = contract_last(go, vn) - row_dot
    ds_c = (p_c.astype(jnp.float32) * g_c * factor).astype(jnp.bfloat16)
    ds_o = (p_o.astype(jnp.float32) * g_o * factor).astype(jnp.bfloat16)
    gq = jnp.dot(ds_c, kc, preferred_element_type=jnp.float32) + jnp.dot(
        ds_o, kn, preferred_element_type=jnp.float32
    )
    gq_ref[...] = gq.astype(jnp.bfloat16)

    @pl.when(member == 0)
    def _():
        gk_acc[...] = jnp.zeros_like(gk_acc)
        gv_acc[...] = jnp.zeros_like(gv_acc)

    gk_acc[...] += contract_first(ds_o, q)
    gv_acc[...] += contract_first(p_o, go)

    @pl.when(member == group - 1)
    def _():
        gk_ref[...] = gk_acc[...].astype(jnp.bfloat16)
        gv_ref[...] = gv_acc[...].astype(jnp.bfloat16)


def attention(starts, proj, key_cache, value_cache, grad_out):
    tokens = proj.shape[0]
    kv_local = key_cache.shape[2] // HD
    cached = key_cache.shape[1]
    group = H // KV
    heads = kv_local * group
    per_head = pl.BlockSpec((tokens, HD), lambda g, m: (0, g * group + m))
    per_kv = pl.BlockSpec((tokens, HD), lambda g, m: (0, g))
    cache = pl.BlockSpec((1, cached, HD), lambda g, m: (0, 0, g))
    bf16 = jnp.bfloat16
    return pl.pallas_call(
        attention_kernel,
        grid=(kv_local, group),
        out_shape=(
            jax.ShapeDtypeStruct((tokens, heads * HD), bf16),
            jax.ShapeDtypeStruct((tokens, heads * HD), bf16),
            jax.ShapeDtypeStruct((tokens, kv_local * HD), bf16),
            jax.ShapeDtypeStruct((tokens, kv_local * HD), bf16),
        ),
        in_specs=[
            pl.BlockSpec(memory_space=pltpu.SMEM),
            per_head,
            pl.BlockSpec((tokens, HD), lambda g, m: (0, heads + g)),
            pl.BlockSpec((tokens, HD), lambda g, m: (0, heads + kv_local + g)),
            cache,
            cache,
            per_head,
        ],
        out_specs=[per_head, per_head, per_kv, per_kv],
        scratch_shapes=[pltpu.VMEM((tokens, HD), jnp.float32)] * 2,
        compiler_params=pltpu.CompilerParams(vmem_limit_bytes=VMEM_LIMIT),
        name="attention",
    )(starts, proj, proj, proj, key_cache, value_cache, grad_out)


def local(blk_count, tp_count, hidden_in, w_query, w_key, w_value, starts, key_cache, value_cache, grad_out):
    tokens_dev, depth = hidden_in.shape
    w = jnp.concatenate([w_query, w_key, w_value], 1)
    full, mate = gather(w, hidden_in, blk_count)
    full = full.reshape(depth, w.shape[1])
    proj = jnp.dot(hidden_in, full, preferred_element_type=jnp.float32).astype(jnp.bfloat16)
    attended, grad_query, grad_keys, grad_values = attention(
        starts, proj, key_cache, value_cache, grad_out
    )
    grads = jnp.concatenate([grad_query, grad_keys, grad_values], 1)
    term = contract_last(grads, full)
    scale = (tokens_dev * blk_count) ** (-0.5)
    summed, others = scatter(
        hidden_in, mate, grads, term.astype(jnp.bfloat16), blk_count, tp_count, scale
    )
    width = depth // tp_count
    grad_in = lax.dynamic_slice_in_dim(term, lax.axis_index("tp") * width, width, 1)
    for k in range(tp_count - 1):
        grad_in = grad_in + others[k].astype(jnp.float32)
    grad_in = grad_in.astype(jnp.bfloat16)
    query_cols, kv_cols = w_query.shape[1], w_key.shape[1]
    return (
        attended,
        grad_in,
        summed[:, :query_cols],
        summed[:, query_cols : query_cols + kv_cols],
        summed[:, query_cols + kv_cols :],
    )


def solution(mesh):
    in_specs = (
        P("blk", None),
        P("blk", "tp"),
        P("blk", "tp"),
        P("blk", "tp"),
        P("blk"),
        P("blk", None, "tp"),
        P("blk", None, "tp"),
        P("blk", "tp"),
    )
    out_specs = (P("blk", "tp"),) * 5
    return jax.shard_map(
        functools.partial(local, mesh.shape["blk"], mesh.shape["tp"]),
        mesh=mesh,
        in_specs=in_specs,
        out_specs=out_specs,
        check_vma=False,
    )
```

```python
import functools

import jax
import jax.numpy as jnp
from jax import lax
from jax.experimental import pallas as pl
from jax.experimental.pallas import tpu as pltpu
from jax.sharding import PartitionSpec as P

H = 32
KV = 8
HD = 128
MESH = pl.DeviceIdType.MESH
LOG2E = 1.4426950408889634
VMEM_LIMIT = 60 * 1024 * 1024


def contract_last(left, right):
    return lax.dot_general(
        left, right, (((1,), (1,)), ((), ())), preferred_element_type=jnp.float32
    )


def contract_first(left, right):
    return lax.dot_general(
        left, right, (((0,), (0,)), ((), ())), preferred_element_type=jnp.float32
    )


def ring_position(chip, n):
    half = n // 2
    if n == 8:
        z, x = chip // 2, chip % 2
    else:
        z, x = chip % half, chip // half
    return z + x * (n - 1 - 2 * z)


def ring_chip(position, n):
    half = n // 2
    x = position // half
    z = position + x * (n - 1 - 2 * position)
    return z * 2 + x if n == 8 else x * half + z


def places(n):
    blk = lax.axis_index("blk")
    core, chip = blk % 2, blk // 2
    position = ring_position(chip, n)

    def device(pos):
        return ring_chip((pos + 2 * n) % n, n) * 2 + core

    return blk, chip * 2 + 1 - core, position, device


def gather_kernel(n, w_ref, hidden_ref, full_ref, pair_ref, hid_send, hid_recv, *sems):
    def exchange(sibling):
        return pltpu.make_async_remote_copy(
            src_ref=hidden_ref, dst_ref=pair_ref, send_sem=hid_send, recv_sem=hid_recv,
            device_id={"blk": sibling}, device_id_type=MESH,
        )

    gather_ring(n, w_ref, full_ref, sems, exchange, None)


def gather_ring(n, w_ref, full_ref, sems, exchange, work):
    own_sem, own_send, own_recv, ring_send, ring_recv, fwd_send, fwd_recv = sems
    blk, sibling, position, device = places(n)
    target = (device(position + 1), device(position - 1))
    quarter = w_ref.shape[0] // 4
    barrier = pltpu.get_barrier_semaphore()
    for other in (sibling,) + target:
        pl.semaphore_signal(barrier, inc=1, device_id={"blk": other}, device_id_type=MESH)
    pl.semaphore_wait(barrier, 3)

    def origin(way, step):
        return device(position - step) if way == 0 else device(position + step)

    def rows(way, k):
        return pl.ds((way * 2 + k) * quarter, quarter)

    def ring_copy(way, k, step, src, index):
        return pltpu.make_async_remote_copy(
            src_ref=src,
            dst_ref=full_ref.at[index, rows(way, k)],
            send_sem=ring_send.at[way, k, step],
            recv_sem=ring_recv.at[way, k, step],
            device_id={"blk": target[way]},
            device_id_type=MESH,
        )

    def forward(way, k, step, index):
        return pltpu.make_async_remote_copy(
            src_ref=full_ref.at[index, rows(way, k)],
            dst_ref=full_ref.at[index, rows(way, k)],
            send_sem=fwd_send.at[way, k, step],
            recv_sem=fwd_recv.at[way, k, step],
            device_id={"blk": sibling},
            device_id_type=MESH,
        )

    for k in range(2):
        for way in range(2):
            ring_copy(way, k, 0, w_ref.at[rows(way, k)], blk).start()
    own = pltpu.make_async_copy(w_ref, full_ref.at[blk], own_sem)
    own.start()
    share = pltpu.make_async_remote_copy(
        src_ref=w_ref, dst_ref=full_ref.at[blk], send_sem=own_send, recv_sem=own_recv,
        device_id={"blk": sibling}, device_id_type=MESH,
    )
    share.start()
    if exchange is not None:
        exchange(sibling).start()

    def step_body(step, carry):
        if work is not None:
            work(step - 1)
        for k in range(2):
            for way in range(2):
                index = origin(way, step)
                here = full_ref.at[index, rows(way, k)]
                ring_copy(way, k, step - 1, here, index).wait_recv()

                @pl.when(step < n - 1)
                def _():
                    ring_copy(way, k, step, here, index).start()

                forward(way, k, step - 1, index).start()
        return carry

    lax.fori_loop(1, n, step_body, 0)

    def drain(step, carry):
        for k in range(2):
            for way in range(2):
                index = origin(way, step)
                here = full_ref.at[index, rows(way, k)]
                ring_copy(way, k, step, here, index).wait_send()
                far = origin(way, step + 1)
                mate = far + sibling - blk
                forward(way, k, step, far).wait_send()
                forward(way, k, step, mate).wait_recv()
        return carry

    lax.fori_loop(0, n - 1, drain, 0)
    own.wait()
    share.wait_send()
    pltpu.make_async_remote_copy(
        src_ref=w_ref, dst_ref=full_ref.at[sibling], send_sem=own_send, recv_sem=own_recv,
        device_id={"blk": sibling}, device_id_type=MESH,
    ).wait_recv()
    if exchange is not None:
        exchange(sibling).wait()


def gather_sems(n):
    dma = pltpu.SemaphoreType.DMA
    return [dma, dma, dma] + [dma((2, 2, n - 1))] * 4


def scatter_scratch(n, tokens, height, width):
    dma = pltpu.SemaphoreType.DMA
    half = width // 2
    return [
        pltpu.VMEM((tokens, width), jnp.bfloat16),
        pltpu.VMEM((2, height, half), jnp.float32),
        pltpu.VMEM((2, n - 1, height, half), jnp.bfloat16),
        pltpu.VMEM((2, n - 1, height, half), jnp.bfloat16),
        dma,
        dma,
        dma((2, 2, n - 1)),
        dma((2, 2, n - 1)),
    ]


def gather(w, hidden, blk_count):
    n = blk_count // 2
    rows, cols = w.shape
    dma = pltpu.SemaphoreType.DMA
    return pl.pallas_call(
        functools.partial(gather_kernel, n),
        out_shape=(
            jax.ShapeDtypeStruct((blk_count, rows, cols), w.dtype),
            jax.ShapeDtypeStruct(hidden.shape, hidden.dtype),
        ),
        in_specs=[pl.BlockSpec(memory_space=pl.ANY)] * 2,
        out_specs=[pl.BlockSpec(memory_space=pl.ANY)] * 2,
        scratch_shapes=[dma, dma] + gather_sems(n),
        compiler_params=pltpu.CompilerParams(collective_id=0, has_side_effects=True),
        name="ring_gather",
    )(w, hidden)


def scatter_kernel(
    n, tp_count, scale, hid_ref, mate_ref, grads_ref, term_ref, out_ref, recv_term_ref,
    term_send, term_recv, *scratch,
):
    chunk = term_ref.shape[1] // tp_count
    tp_me = lax.axis_index("tp")

    def copy(k):
        peer = (tp_me + k) % tp_count
        return pltpu.make_async_remote_copy(
            src_ref=term_ref.at[:, pl.ds(pl.multiple_of(peer * chunk, 128), chunk)],
            dst_ref=recv_term_ref.at[k - 1],
            send_sem=term_send.at[k - 1],
            recv_sem=term_recv.at[k - 1],
            device_id={"tp": peer},
            device_id_type=MESH,
        )

    def before():
        for k in range(1, tp_count):
            copy(k).start()

    scatter_ring(
        n, tp_count, scale, hid_ref, mate_ref, grads_ref, out_ref, scratch, before, None
    )
    for k in range(1, tp_count):
        copy(k).wait()


def scatter_ring(
    n, tp_greet, scale, hid_ref, mate_ref, grads_ref, out_ref, scratch, before, work
):
    mate_grads, part, send_buf, recv_buf, gr_send, gr_recv, ring_send, ring_recv = scratch
    blk, sibling, position, device = places(n)
    target = (device(position + 1), device(position - 1))
    height, width = out_ref.shape
    half_rows, half = height // 2, width // 2
    tile = 384 if half % 384 == 0 else 128
    barrier = pltpu.get_barrier_semaphore()
    for other in (sibling,) + target:
        pl.semaphore_signal(barrier, inc=1, device_id={"blk": other}, device_id_type=MESH)
    for k in range(1, tp_greet):
        peer = (lax.axis_index("tp") + k) % tp_greet
        pl.semaphore_signal(barrier, inc=1, device_id={"tp": peer}, device_id_type=MESH)
    pl.semaphore_wait(barrier, 3 + tp_greet - 1)

    share = pltpu.make_async_remote_copy(
        src_ref=grads_ref, dst_ref=mate_grads, send_sem=gr_send, recv_sem=gr_recv,
        device_id={"blk": sibling}, device_id_type=MESH,
    )
    share.start()
    if before is not None:
        before()
    share.wait()

    def ring_copy(way, k, step):
        spot = pl.ds(k * half_rows, half_rows)
        return pltpu.make_async_remote_copy(
            src_ref=send_buf.at[way, step, spot],
            dst_ref=recv_buf.at[way, step, spot],
            send_sem=ring_send.at[way, k, step],
            recv_sem=ring_recv.at[way, k, step],
            device_id={"blk": target[way]},
            device_id_type=MESH,
        )

    def step_body(step, carry):
        for way in range(2):
            owner = device(position - 1 - step) if way == 0 else device(position + 1 + step)
            columns = pl.ds(pl.multiple_of(owner * height, 128), height)

            def tile_body(t, inner):
                at = pl.multiple_of(way * half + t * tile, 128)
                to = pl.multiple_of(t * tile, 128)
                part[way, :, pl.ds(to, tile)] = contract_first(
                    hid_ref[:, columns], grads_ref[:, pl.ds(at, tile)]
                ) + contract_first(mate_ref[:, columns], mate_grads[:, pl.ds(at, tile)])
                return inner

            lax.fori_loop(0, half // tile, tile_body, 0)
        for k in range(2):
            for way in range(2):
                spot = pl.ds(k * half_rows, half_rows)

                @pl.when(step > 0)
                def _():
                    ring_copy(way, k, step - 1).wait_recv()
                    part[way, spot] += recv_buf[way, step - 1, spot].astype(jnp.float32)

                @pl.when(step < n - 1)
                def _():
                    send_buf[way, step, spot] = part[way, spot].astype(jnp.bfloat16)
                    ring_copy(way, k, step).start()

        if work is not None:
            work(step)
        return carry

    lax.fori_loop(0, n, step_body, 0)
    for way in range(2):
        out_ref[:, way * half : (way + 1) * half] = part[way] * scale

    def drain(step, carry):
        for k in range(2):
            for way in range(2):
                ring_copy(way, k, step).wait_send()
        return carry

    lax.fori_loop(0, n - 1, drain, 0)


def scatter(hidden, mate, grads, term, blk_count, tp_count, scale):
    n = blk_count // 2
    tokens, depth = hidden.shape
    height, width = depth // blk_count, grads.shape[1]
    dma = pltpu.SemaphoreType.DMA
    vmem = pl.BlockSpec(memory_space=pltpu.VMEM)
    hbm = pl.BlockSpec(memory_space=pl.ANY)
    return pl.pallas_call(
        functools.partial(scatter_kernel, n, tp_count, scale),
        out_shape=(
            jax.ShapeDtypeStruct((height, width), jnp.float32),
            jax.ShapeDtypeStruct((tp_count - 1, tokens, depth // tp_count), jnp.bfloat16),
        ),
        in_specs=[vmem, vmem, vmem, hbm],
        out_specs=[vmem, hbm],
        scratch_shapes=[dma((tp_count - 1,)), dma((tp_count - 1,))]
        + scatter_scratch(n, tokens, height, width),
        compiler_params=pltpu.CompilerParams(
            collective_id=1, has_side_effects=True, vmem_limit_bytes=VMEM_LIMIT
        ),
        name="ring_scatter",
    )(hidden, mate, grads, term)


def attention_kernel(
    starts_ref, q_ref, kn_ref, vn_ref, kc_ref, vc_ref, go_ref,
    att_ref, gq_ref, gk_ref, gv_ref, gk_acc, gv_acc,
):
    member, group = pl.program_id(1), pl.num_programs(1)
    rows, cached = q_ref.shape[0], kc_ref.shape[1]
    factor = HD ** (-0.5)
    q, go = q_ref[...], go_ref[...]
    kn, vn, kc, vc = kn_ref[...], vn_ref[...], kc_ref[0], vc_ref[0]
    slot = lax.broadcasted_iota(jnp.int32, (rows, cached), 1)
    s_c = jnp.where(slot < starts_ref[0], contract_last(q, kc), -jnp.inf)
    row = lax.broadcasted_iota(jnp.int32, (rows, rows), 0)
    col = lax.broadcasted_iota(jnp.int32, (rows, rows), 1)
    s_o = jnp.where(col <= row, contract_last(q, kn), -jnp.inf)
    top = jnp.maximum(
        jnp.max(s_c, axis=-1, keepdims=True), jnp.max(s_o, axis=-1, keepdims=True)
    )
    e_c = jnp.exp2((s_c - top) * (factor * LOG2E))
    e_o = jnp.exp2((s_o - top) * (factor * LOG2E))
    total = jnp.sum(e_c, axis=-1, keepdims=True) + jnp.sum(e_o, axis=-1, keepdims=True)
    inverse = 1.0 / total
    p_c = (e_c * inverse).astype(jnp.bfloat16)
    p_o = (e_o * inverse).astype(jnp.bfloat16)
    att = jnp.dot(p_c, vc, preferred_element_type=jnp.float32) + jnp.dot(
        p_o, vn, preferred_element_type=jnp.float32
    )
    att_ref[...] = att.astype(jnp.bfloat16)
    row_dot = jnp.sum(att * go.astype(jnp.float32), axis=-1, keepdims=True)
    g_c = contract_last(go, vc) - row_dot
    g_o = contract_last(go, vn) - row_dot
    ds_c = (p_c.astype(jnp.float32) * g_c * factor).astype(jnp.bfloat16)
    ds_o = (p_o.astype(jnp.float32) * g_o * factor).astype(jnp.bfloat16)
    gq = jnp.dot(ds_c, kc, preferred_element_type=jnp.float32) + jnp.dot(
        ds_o, kn, preferred_element_type=jnp.float32
    )
    gq_ref[...] = gq.astype(jnp.bfloat16)

    @pl.when(member == 0)
    def _():
        gk_acc[...] = jnp.zeros_like(gk_acc)
        gv_acc[...] = jnp.zeros_like(gv_acc)

    gk_acc[...] += contract_first(ds_o, q)
    gv_acc[...] += contract_first(p_o, go)

    @pl.when(member == group - 1)
    def _():
        gk_ref[...] = gk_acc[...].astype(jnp.bfloat16)
        gv_ref[...] = gv_acc[...].astype(jnp.bfloat16)


def attention(starts, proj, key_cache, value_cache, grad_out):
    tokens = proj.shape[0]
    kv_local = key_cache.shape[2] // HD
    cached = key_cache.shape[1]
    group = H // KV
    heads = kv_local * group
    per_head = pl.BlockSpec((tokens, HD), lambda g, m: (0, g * group + m))
    per_kv = pl.BlockSpec((tokens, HD), lambda g, m: (0, g))
    cache = pl.BlockSpec((1, cached, HD), lambda g, m: (0, 0, g))
    bf16 = jnp.bfloat16
    return pl.pallas_call(
        attention_kernel,
        grid=(kv_local, group),
        out_shape=(
            jax.ShapeDtypeStruct((tokens, heads * HD), bf16),
            jax.ShapeDtypeStruct((tokens, heads * HD), bf16),
            jax.ShapeDtypeStruct((tokens, kv_local * HD), bf16),
            jax.ShapeDtypeStruct((tokens, kv_local * HD), bf16),
        ),
        in_specs=[
            pl.BlockSpec(memory_space=pltpu.SMEM),
            per_head,
            pl.BlockSpec((tokens, HD), lambda g, m: (0, heads + g)),
            pl.BlockSpec((tokens, HD), lambda g, m: (0, heads + kv_local + g)),
            cache,
            cache,
            per_head,
        ],
        out_specs=[per_head, per_head, per_kv, per_kv],
        scratch_shapes=[pltpu.VMEM((tokens, HD), jnp.float32)] * 2,
        compiler_params=pltpu.CompilerParams(vmem_limit_bytes=VMEM_LIMIT),
        name="attention",
    )(starts, proj, proj, proj, key_cache, value_cache, grad_out)


def head_work(heads, group, per_step, ins, outs, accs):
    bias_ref, proj_ref, kc_ref, vc_ref, go_ref = ins
    att_ref, grads_ref = outs
    gk_acc, gv_acc = accs
    kvs = heads // group
    key_at, value_at = heads * HD, (heads + kvs) * HD
    factor = HD ** (-0.5)
    rows = proj_ref.shape[0]

    def one(head):
        g = head // group
        q_cols = pl.ds(pl.multiple_of(head * HD, HD), HD)
        kv_cols = pl.ds(pl.multiple_of(g * HD, HD), HD)
        q, go = proj_ref[:, q_cols], go_ref[:, q_cols]
        kn = proj_ref[:, pl.ds(pl.multiple_of(key_at + g * HD, HD), HD)]
        vn = proj_ref[:, pl.ds(pl.multiple_of(value_at + g * HD, HD), HD)]
        kc, vc = kc_ref[:, kv_cols], vc_ref[:, kv_cols]
        s_c = contract_last(q, kc) + bias_ref[...]
        row = lax.broadcasted_iota(jnp.int32, (rows, rows), 0)
        col = lax.broadcasted_iota(jnp.int32, (rows, rows), 1)
        s_o = jnp.where(col <= row, contract_last(q, kn), -jnp.inf)
        top = jnp.maximum(
            jnp.max(s_c, axis=-1, keepdims=True), jnp.max(s_o, axis=-1, keepdims=True)
        )
        e_c = jnp.exp2((s_c - top) * (factor * LOG2E))
        e_o = jnp.exp2((s_o - top) * (factor * LOG2E))
        total = jnp.sum(e_c, axis=-1, keepdims=True) + jnp.sum(e_o, axis=-1, keepdims=True)
        inverse = 1.0 / total
        p_c = (e_c * inverse).astype(jnp.bfloat16)
        p_o = (e_o * inverse).astype(jnp.bfloat16)
        att = jnp.dot(p_c, vc, preferred_element_type=jnp.float32) + jnp.dot(
            p_o, vn, preferred_element_type=jnp.float32
        )
        att_ref[:, q_cols] = att.astype(jnp.bfloat16)
        row_dot = jnp.sum(att * go.astype(jnp.float32), axis=-1, keepdims=True)
        g_c = contract_last(go, vc) - row_dot
        g_o = contract_last(go, vn) - row_dot
        ds_c = (p_c.astype(jnp.float32) * g_c * factor).astype(jnp.bfloat16)
        ds_o = (p_o.astype(jnp.float32) * g_o * factor).astype(jnp.bfloat16)
        gq = jnp.dot(ds_c, kc, preferred_element_type=jnp.float32) + jnp.dot(
            ds_o, kn, preferred_element_type=jnp.float32
        )
        grads_ref[:, q_cols] = gq.astype(jnp.bfloat16)
        gk_acc[g] += contract_first(ds_o, q)
        gv_acc[g] += contract_first(p_o, go)

    def work(step):
        def each(j, carry):
            head = step * per_step + j

            @pl.when(head < heads)
            def _():
                one(head)

            return carry

        lax.fori_loop(0, per_step, each, 0)

    def finish():
        for g in range(kvs):
            grads_ref[:, key_at + g * HD : key_at + (g + 1) * HD] = gk_acc[g].astype(jnp.bfloat16)
            grads_ref[:, value_at + g * HD : value_at + (g + 1) * HD] = gv_acc[g].astype(
                jnp.bfloat16
            )

    gk_acc[...] = jnp.zeros_like(gk_acc)
    gv_acc[...] = jnp.zeros_like(gv_acc)
    return work, finish


def gather_attend_kernel(
    n, heads, group, w_ref, bias_ref, proj_ref, kc_ref, vc_ref, go_ref,
    full_ref, att_ref, grads_ref, gk_acc, gv_acc, *sems,
):
    work, finish = head_work(
        heads, group, -(-heads // (n - 1)), (bias_ref, proj_ref, kc_ref, vc_ref, go_ref),
        (att_ref, grads_ref), (gk_acc, gv_acc),
    )
    gather_ring(n, w_ref, full_ref, sems, None, work)
    finish()


def scatter_attend_kernel(
    n, heads, group, scale, hid_ref, mate_ref, done_ref, bias_ref, proj_ref, kc_ref, vc_ref,
    go_ref, out_ref, att_ref, grads_ref, gk_acc, gv_acc, *scratch,
):
    work, finish = head_work(
        heads, group, -(-heads // (n - 1)), (bias_ref, proj_ref, kc_ref, vc_ref, go_ref),
        (att_ref, grads_ref), (gk_acc, gv_acc),
    )
    scatter_ring(n, 1, scale, hid_ref, mate_ref, done_ref, out_ref, scratch, None, work)
    finish()


def scatter_input_kernel(
    n, scale, hid_ref, mate_ref, first_ref, second_ref, wa_ref, wb_ref, out_ref, gin_ref,
    wa_buf, wb_buf, own, term, mate_term, wa_sem, wb_sem, term_send, term_recv, *scratch,
):
    tp_me = lax.axis_index("tp")
    span = wa_buf.shape[1]
    steps = n // 2

    def load(c):
        first_row = ((tp_me + 1 + c // steps) % 2) * (steps * span) + (c % steps) * span
        at = pl.ds(pl.multiple_of(first_row, 128), span)
        slot = c % 2
        return (
            pltpu.make_async_copy(wa_ref.at[at], wa_buf.at[slot], wa_sem.at[slot]),
            pltpu.make_async_copy(wb_ref.at[at], wb_buf.at[slot], wb_sem.at[slot]),
        )

    def send():
        return pltpu.make_async_remote_copy(
            src_ref=term, dst_ref=mate_term, send_sem=term_send, recv_sem=term_recv,
            device_id={"tp": (tp_me + 1) % 2}, device_id_type=MESH,
        )

    def before():
        for copy in load(0):
            copy.start()

    def work(step):
        @pl.when(step < n - 1)
        def _():
            for copy in load(step + 1):
                copy.start()

        for copy in load(step):
            copy.wait()
        value = contract_last(first_ref[...], wa_buf[step % 2]) + contract_last(
            second_ref[...], wb_buf[step % 2]
        )
        at = pl.ds(pl.multiple_of((step % steps) * span, 128), span)

        @pl.when(step < steps)
        def _():
            term[:, at] = value.astype(jnp.bfloat16)

        @pl.when(step >= steps)
        def _():
            own[:, at] = value

        @pl.when(step == steps - 1)
        def _():
            send().start()

    scatter_ring(n, 2, scale, hid_ref, mate_ref, second_ref, out_ref, scratch, before, work)
    send().wait()
    gin_ref[...] = (own[...] + mate_term[...].astype(jnp.float32)).astype(jnp.bfloat16)


def in_phases(blk_count, hidden, w_query, w_key, w_value, starts, key_cache, value_cache, grad_out):
    n = blk_count // 2
    tokens, depth = hidden.shape
    height, cached, group = depth // blk_count, key_cache.shape[1], H // KV
    kvs = w_key.shape[1] // HD // 2
    heads = kvs * group
    q_cols, kv_cols = heads * HD, kvs * HD
    width = q_cols + 2 * kv_cols
    scale = (tokens * blk_count) ** (-0.5)
    f32, bf16 = jnp.float32, jnp.bfloat16
    dma = pltpu.SemaphoreType.DMA
    vmem = pl.BlockSpec(memory_space=pltpu.VMEM)
    hbm = pl.BlockSpec(memory_space=pl.ANY)
    shape = jax.ShapeDtypeStruct

    def cut(i):
        kv = slice(i * kv_cols, (i + 1) * kv_cols)
        qs = slice(i * q_cols, (i + 1) * q_cols)
        w = jnp.concatenate([w_query[:, qs], w_key[:, kv], w_value[:, kv]], 1)
        return w, key_cache[0, :, kv], value_cache[0, :, kv], grad_out[:, qs]

    def params(number):
        return pltpu.CompilerParams(
            collective_id=number, has_side_effects=True, vmem_limit_bytes=VMEM_LIMIT
        )

    def project(full):
        return jnp.dot(hidden, full, preferred_element_type=f32).astype(bf16)

    slots = lax.broadcasted_iota(jnp.int32, (1, cached), 1)
    bias = jnp.where(slots < starts[0], 0.0, -jnp.inf).astype(f32)
    accs = [pltpu.VMEM((kvs, tokens, HD), f32)] * 2
    w_a, kc_a, vc_a, go_a = cut(0)
    w_b, kc_b, vc_b, go_b = cut(1)
    full_a, mate = gather(w_a, hidden, blk_count)
    full_a = full_a.reshape(depth, width)
    full_b, att_a, grads_a = pl.pallas_call(
        functools.partial(gather_attend_kernel, n, heads, group),
        out_shape=(
            shape((blk_count, height, width), bf16),
            shape((tokens, q_cols), bf16),
            shape((tokens, width), bf16),
        ),
        in_specs=[hbm] + [vmem] * 5,
        out_specs=[hbm, vmem, vmem],
        scratch_shapes=accs + gather_sems(n),
        compiler_params=params(1),
        name="gather_attend",
    )(w_b, bias, project(full_a), kc_a, vc_a, go_a)
    full_b = full_b.reshape(depth, width)
    sum_a, att_b, grads_b = pl.pallas_call(
        functools.partial(scatter_attend_kernel, n, heads, group, scale),
        out_shape=(
            shape((height, width), f32),
            shape((tokens, q_cols), bf16),
            shape((tokens, width), bf16),
        ),
        in_specs=[vmem] * 8,
        out_specs=[vmem] * 3,
        scratch_shapes=accs + scatter_scratch(n, tokens, height, width),
        compiler_params=params(2),
        name="scatter_attend",
    )(hidden, mate, grads_a, bias, project(full_b), kc_b, vc_b, go_b)
    sum_b, grad_in = pl.pallas_call(
        functools.partial(scatter_input_kernel, n, scale),
        out_shape=(shape((height, width), f32), shape((tokens, depth // 2), bf16)),
        in_specs=[vmem] * 4 + [hbm] * 2,
        out_specs=[vmem] * 2,
        scratch_shapes=[
            pltpu.VMEM((2, depth // n, width), bf16),
            pltpu.VMEM((2, depth // n, width), bf16),
            pltpu.VMEM((tokens, depth // 2), f32),
            pltpu.VMEM((tokens, depth // 2), bf16),
            pltpu.VMEM((tokens, depth // 2), bf16),
            dma((2,)),
            dma((2,)),
            dma,
            dma,
        ]
        + scatter_scratch(n, tokens, height, width),
        compiler_params=params(3),
        name="scatter_input",
    )(hidden, mate, grads_a, grads_b, full_a, full_b)

    def join(first, last):
        return jnp.concatenate([sum_a[:, first:last], sum_b[:, first:last]], 1)

    return (
        jnp.concatenate([att_a, att_b], 1),
        grad_in,
        join(0, q_cols),
        join(q_cols, q_cols + kv_cols),
        join(q_cols + kv_cols, width),
    )


def local(blk_count, tp_count, hidden_in, w_query, w_key, w_value, starts, key_cache, value_cache, grad_out):
    tokens_dev, depth = hidden_in.shape
    if tp_count == 2 and (w_key.shape[1] // HD) % 2 == 0 and blk_count % 4 == 0:
        return in_phases(
            blk_count, hidden_in, w_query, w_key, w_value, starts, key_cache, value_cache, grad_out
        )
    w = jnp.concatenate([w_query, w_key, w_value], 1)
    full, mate = gather(w, hidden_in, blk_count)
    full = full.reshape(depth, w.shape[1])
    proj = jnp.dot(hidden_in, full, preferred_element_type=jnp.float32).astype(jnp.bfloat16)
    attended, grad_query, grad_keys, grad_values = attention(
        starts, proj, key_cache, value_cache, grad_out
    )
    grads = jnp.concatenate([grad_query, grad_keys, grad_values], 1)
    term = contract_last(grads, full)
    scale = (tokens_dev * blk_count) ** (-0.5)
    summed, others = scatter(
        hidden_in, mate, grads, term.astype(jnp.bfloat16), blk_count, tp_count, scale
    )
    width = depth // tp_count
    grad_in = lax.dynamic_slice_in_dim(term, lax.axis_index("tp") * width, width, 1)
    for k in range(tp_count - 1):
        grad_in = grad_in + others[k].astype(jnp.float32)
    grad_in = grad_in.astype(jnp.bfloat16)
    query_cols, kv_cols = w_query.shape[1], w_key.shape[1]
    return (
        attended,
        grad_in,
        summed[:, :query_cols],
        summed[:, query_cols : query_cols + kv_cols],
        summed[:, query_cols + kv_cols :],
    )


def solution(mesh):
    in_specs = (
        P("blk", None),
        P("blk", "tp"),
        P("blk", "tp"),
        P("blk", "tp"),
        P("blk"),
        P("blk", None, "tp"),
        P("blk", None, "tp"),
        P("blk", "tp"),
    )
    out_specs = (P("blk", "tp"),) * 5
    return jax.shard_map(
        functools.partial(local, mesh.shape["blk"], mesh.shape["tp"]),
        mesh=mesh,
        in_specs=in_specs,
        out_specs=out_specs,
        check_vma=False,
    )
```

```python
import functools

import jax
import jax.numpy as jnp
from jax import lax
from jax.experimental import pallas as pl
from jax.experimental.pallas import tpu as pltpu
from jax.sharding import PartitionSpec as P

H = 32
KV = 8
HD = 128
MESH = pl.DeviceIdType.MESH
LOG2E = 1.4426950408889634
VMEM_LIMIT = 60 * 1024 * 1024


def contract_last(left, right):
    return lax.dot_general(
        left, right, (((1,), (1,)), ((), ())), preferred_element_type=jnp.float32
    )


def contract_first(left, right):
    return lax.dot_general(
        left, right, (((0,), (0,)), ((), ())), preferred_element_type=jnp.float32
    )


def ring_position(chip, n):
    half = n // 2
    if n == 8:
        z, x = chip // 2, chip % 2
    else:
        z, x = chip % half, chip // half
    return z + x * (n - 1 - 2 * z)


def ring_chip(position, n):
    half = n // 2
    x = position // half
    z = position + x * (n - 1 - 2 * position)
    return z * 2 + x if n == 8 else x * half + z


def places(n):
    blk = lax.axis_index("blk")
    core, chip = blk % 2, blk // 2
    position = ring_position(chip, n)

    def device(pos):
        return ring_chip((pos + 2 * n) % n, n) * 2 + core

    return blk, chip * 2 + 1 - core, position, device


def gather_kernel(n, w_ref, hidden_ref, full_ref, pair_ref, hid_send, hid_recv, *sems):
    def exchange(sibling):
        return pltpu.make_async_remote_copy(
            src_ref=hidden_ref, dst_ref=pair_ref, send_sem=hid_send, recv_sem=hid_recv,
            device_id={"blk": sibling}, device_id_type=MESH,
        )

    gather_ring(n, w_ref, full_ref, sems, exchange, None)


def gather_ring(n, w_ref, full_ref, sems, exchange, work):
    own_sem, own_send, own_recv, ring_send, ring_recv, fwd_send, fwd_recv = sems
    blk, sibling, position, device = places(n)
    target = (device(position + 1), device(position - 1))
    quarter = w_ref.shape[0] // 4
    barrier = pltpu.get_barrier_semaphore()
    for other in (sibling,) + target:
        pl.semaphore_signal(barrier, inc=1, device_id={"blk": other}, device_id_type=MESH)
    pl.semaphore_wait(barrier, 3)

    def origin(way, step):
        return device(position - step) if way == 0 else device(position + step)

    def rows(way, k):
        return pl.ds((way * 2 + k) * quarter, quarter)

    def ring_copy(way, k, step, src, index):
        return pltpu.make_async_remote_copy(
            src_ref=src,
            dst_ref=full_ref.at[index, rows(way, k)],
            send_sem=ring_send.at[way, k, step],
            recv_sem=ring_recv.at[way, k, step],
            device_id={"blk": target[way]},
            device_id_type=MESH,
        )

    def forward(way, k, step, index):
        return pltpu.make_async_remote_copy(
            src_ref=full_ref.at[index, rows(way, k)],
            dst_ref=full_ref.at[index, rows(way, k)],
            send_sem=fwd_send.at[way, k, step],
            recv_sem=fwd_recv.at[way, k, step],
            device_id={"blk": sibling},
            device_id_type=MESH,
        )

    for k in range(2):
        for way in range(2):
            ring_copy(way, k, 0, w_ref.at[rows(way, k)], blk).start()
    own = pltpu.make_async_copy(w_ref, full_ref.at[blk], own_sem)
    own.start()
    share = pltpu.make_async_remote_copy(
        src_ref=w_ref, dst_ref=full_ref.at[blk], send_sem=own_send, recv_sem=own_recv,
        device_id={"blk": sibling}, device_id_type=MESH,
    )
    share.start()
    if exchange is not None:
        exchange(sibling).start()

    def step_body(step, carry):
        if work is not None:
            work(step - 1)
        for k in range(2):
            for way in range(2):
                index = origin(way, step)
                here = full_ref.at[index, rows(way, k)]
                ring_copy(way, k, step - 1, here, index).wait_recv()

                @pl.when(step < n - 1)
                def _():
                    ring_copy(way, k, step, here, index).start()

                forward(way, k, step - 1, index).start()
        return carry

    lax.fori_loop(1, n, step_body, 0)

    def drain(step, carry):
        for k in range(2):
            for way in range(2):
                index = origin(way, step)
                here = full_ref.at[index, rows(way, k)]
                ring_copy(way, k, step, here, index).wait_send()
                far = origin(way, step + 1)
                mate = far + sibling - blk
                forward(way, k, step, far).wait_send()
                forward(way, k, step, mate).wait_recv()
        return carry

    lax.fori_loop(0, n - 1, drain, 0)
    own.wait()
    share.wait_send()
    pltpu.make_async_remote_copy(
        src_ref=w_ref, dst_ref=full_ref.at[sibling], send_sem=own_send, recv_sem=own_recv,
        device_id={"blk": sibling}, device_id_type=MESH,
    ).wait_recv()
    if exchange is not None:
        exchange(sibling).wait()


def gather_sems(n):
    dma = pltpu.SemaphoreType.DMA
    return [dma, dma, dma] + [dma((2, 2, n - 1))] * 4


def scatter_scratch(n, tokens, height, width):
    dma = pltpu.SemaphoreType.DMA
    half = width // 2
    return [
        pltpu.VMEM((tokens, width), jnp.bfloat16),
        pltpu.VMEM((2, height, half), jnp.float32),
        pltpu.VMEM((2, n - 1, height, half), jnp.bfloat16),
        pltpu.VMEM((2, n - 1, height, half), jnp.bfloat16),
        dma,
        dma,
        dma((2, 2, n - 1)),
        dma((2, 2, n - 1)),
    ]


def gather(w, hidden, blk_count):
    n = blk_count // 2
    rows, cols = w.shape
    dma = pltpu.SemaphoreType.DMA
    return pl.pallas_call(
        functools.partial(gather_kernel, n),
        out_shape=(
            jax.ShapeDtypeStruct((blk_count, rows, cols), w.dtype),
            jax.ShapeDtypeStruct(hidden.shape, hidden.dtype),
        ),
        in_specs=[pl.BlockSpec(memory_space=pl.ANY)] * 2,
        out_specs=[pl.BlockSpec(memory_space=pl.ANY)] * 2,
        scratch_shapes=[dma, dma] + gather_sems(n),
        compiler_params=pltpu.CompilerParams(collective_id=0, has_side_effects=True),
        name="ring_gather",
    )(w, hidden)


def scatter_kernel(
    n, tp_count, scale, hid_ref, mate_ref, grads_ref, term_ref, out_ref, recv_term_ref,
    term_send, term_recv, *scratch,
):
    chunk = term_ref.shape[1] // tp_count
    tp_me = lax.axis_index("tp")

    def copy(k):
        peer = (tp_me + k) % tp_count
        return pltpu.make_async_remote_copy(
            src_ref=term_ref.at[:, pl.ds(pl.multiple_of(peer * chunk, 128), chunk)],
            dst_ref=recv_term_ref.at[k - 1],
            send_sem=term_send.at[k - 1],
            recv_sem=term_recv.at[k - 1],
            device_id={"tp": peer},
            device_id_type=MESH,
        )

    def before():
        for k in range(1, tp_count):
            copy(k).start()

    scatter_ring(
        n, tp_count, scale, hid_ref, mate_ref, grads_ref, out_ref, scratch, before, None
    )
    for k in range(1, tp_count):
        copy(k).wait()


def scatter_ring(
    n, tp_greet, scale, hid_ref, mate_ref, grads_ref, out_ref, scratch, before, work
):
    mate_grads, part, send_buf, recv_buf, gr_send, gr_recv, ring_send, ring_recv = scratch
    blk, sibling, position, device = places(n)
    target = (device(position + 1), device(position - 1))
    height, width = out_ref.shape
    half_rows, half = height // 2, width // 2
    tile = 384 if half % 384 == 0 else 128
    barrier = pltpu.get_barrier_semaphore()
    for other in (sibling,) + target:
        pl.semaphore_signal(barrier, inc=1, device_id={"blk": other}, device_id_type=MESH)
    for k in range(1, tp_greet):
        peer = (lax.axis_index("tp") + k) % tp_greet
        pl.semaphore_signal(barrier, inc=1, device_id={"tp": peer}, device_id_type=MESH)
    pl.semaphore_wait(barrier, 3 + tp_greet - 1)

    share = pltpu.make_async_remote_copy(
        src_ref=grads_ref, dst_ref=mate_grads, send_sem=gr_send, recv_sem=gr_recv,
        device_id={"blk": sibling}, device_id_type=MESH,
    )
    share.start()
    if before is not None:
        before()
    share.wait()

    def ring_copy(way, k, step):
        spot = pl.ds(k * half_rows, half_rows)
        return pltpu.make_async_remote_copy(
            src_ref=send_buf.at[way, step, spot],
            dst_ref=recv_buf.at[way, step, spot],
            send_sem=ring_send.at[way, k, step],
            recv_sem=ring_recv.at[way, k, step],
            device_id={"blk": target[way]},
            device_id_type=MESH,
        )

    def step_body(step, carry):
        for way in range(2):
            owner = device(position - 1 - step) if way == 0 else device(position + 1 + step)
            columns = pl.ds(pl.multiple_of(owner * height, 128), height)

            def tile_body(t, inner):
                at = pl.multiple_of(way * half + t * tile, 128)
                to = pl.multiple_of(t * tile, 128)
                part[way, :, pl.ds(to, tile)] = contract_first(
                    hid_ref[:, columns], grads_ref[:, pl.ds(at, tile)]
                ) + contract_first(mate_ref[:, columns], mate_grads[:, pl.ds(at, tile)])
                return inner

            lax.fori_loop(0, half // tile, tile_body, 0)
        for k in range(2):
            for way in range(2):
                spot = pl.ds(k * half_rows, half_rows)

                @pl.when(step > 0)
                def _():
                    ring_copy(way, k, step - 1).wait_recv()
                    part[way, spot] += recv_buf[way, step - 1, spot].astype(jnp.float32)

                @pl.when(step < n - 1)
                def _():
                    send_buf[way, step, spot] = part[way, spot].astype(jnp.bfloat16)
                    ring_copy(way, k, step).start()

        if work is not None:
            work(step)
        return carry

    lax.fori_loop(0, n, step_body, 0)
    for way in range(2):
        out_ref[:, way * half : (way + 1) * half] = part[way] * scale

    def drain(step, carry):
        for k in range(2):
            for way in range(2):
                ring_copy(way, k, step).wait_send()
        return carry

    lax.fori_loop(0, n - 1, drain, 0)


def scatter(hidden, mate, grads, term, blk_count, tp_count, scale):
    n = blk_count // 2
    tokens, depth = hidden.shape
    height, width = depth // blk_count, grads.shape[1]
    dma = pltpu.SemaphoreType.DMA
    vmem = pl.BlockSpec(memory_space=pltpu.VMEM)
    hbm = pl.BlockSpec(memory_space=pl.ANY)
    return pl.pallas_call(
        functools.partial(scatter_kernel, n, tp_count, scale),
        out_shape=(
            jax.ShapeDtypeStruct((height, width), jnp.float32),
            jax.ShapeDtypeStruct((tp_count - 1, tokens, depth // tp_count), jnp.bfloat16),
        ),
        in_specs=[vmem, vmem, vmem, hbm],
        out_specs=[vmem, hbm],
        scratch_shapes=[dma((tp_count - 1,)), dma((tp_count - 1,))]
        + scatter_scratch(n, tokens, height, width),
        compiler_params=pltpu.CompilerParams(
            collective_id=1, has_side_effects=True, vmem_limit_bytes=VMEM_LIMIT
        ),
        name="ring_scatter",
    )(hidden, mate, grads, term)


def attention_kernel(
    starts_ref, q_ref, kn_ref, vn_ref, kc_ref, vc_ref, go_ref,
    att_ref, gq_ref, gk_ref, gv_ref, gk_acc, gv_acc,
):
    member, group = pl.program_id(1), pl.num_programs(1)
    rows, cached = q_ref.shape[0], kc_ref.shape[1]
    factor = HD ** (-0.5)
    q, go = q_ref[...], go_ref[...]
    kn, vn, kc, vc = kn_ref[...], vn_ref[...], kc_ref[0], vc_ref[0]
    slot = lax.broadcasted_iota(jnp.int32, (rows, cached), 1)
    s_c = jnp.where(slot < starts_ref[0], contract_last(q, kc), -jnp.inf)
    row = lax.broadcasted_iota(jnp.int32, (rows, rows), 0)
    col = lax.broadcasted_iota(jnp.int32, (rows, rows), 1)
    s_o = jnp.where(col <= row, contract_last(q, kn), -jnp.inf)
    top = jnp.maximum(
        jnp.max(s_c, axis=-1, keepdims=True), jnp.max(s_o, axis=-1, keepdims=True)
    )
    e_c = jnp.exp2((s_c - top) * (factor * LOG2E))
    e_o = jnp.exp2((s_o - top) * (factor * LOG2E))
    total = jnp.sum(e_c, axis=-1, keepdims=True) + jnp.sum(e_o, axis=-1, keepdims=True)
    inverse = 1.0 / total
    p_c = (e_c * inverse).astype(jnp.bfloat16)
    p_o = (e_o * inverse).astype(jnp.bfloat16)
    att = jnp.dot(p_c, vc, preferred_element_type=jnp.float32) + jnp.dot(
        p_o, vn, preferred_element_type=jnp.float32
    )
    att_ref[...] = att.astype(jnp.bfloat16)
    row_dot = jnp.sum(att * go.astype(jnp.float32), axis=-1, keepdims=True)
    g_c = contract_last(go, vc) - row_dot
    g_o = contract_last(go, vn) - row_dot
    ds_c = (p_c.astype(jnp.float32) * g_c * factor).astype(jnp.bfloat16)
    ds_o = (p_o.astype(jnp.float32) * g_o * factor).astype(jnp.bfloat16)
    gq = jnp.dot(ds_c, kc, preferred_element_type=jnp.float32) + jnp.dot(
        ds_o, kn, preferred_element_type=jnp.float32
    )
    gq_ref[...] = gq.astype(jnp.bfloat16)

    @pl.when(member == 0)
    def _():
        gk_acc[...] = jnp.zeros_like(gk_acc)
        gv_acc[...] = jnp.zeros_like(gv_acc)

    gk_acc[...] += contract_first(ds_o, q)
    gv_acc[...] += contract_first(p_o, go)

    @pl.when(member == group - 1)
    def _():
        gk_ref[...] = gk_acc[...].astype(jnp.bfloat16)
        gv_ref[...] = gv_acc[...].astype(jnp.bfloat16)


def attention(starts, proj, key_cache, value_cache, grad_out):
    tokens = proj.shape[0]
    kv_local = key_cache.shape[2] // HD
    cached = key_cache.shape[1]
    group = H // KV
    heads = kv_local * group
    per_head = pl.BlockSpec((tokens, HD), lambda g, m: (0, g * group + m))
    per_kv = pl.BlockSpec((tokens, HD), lambda g, m: (0, g))
    cache = pl.BlockSpec((1, cached, HD), lambda g, m: (0, 0, g))
    bf16 = jnp.bfloat16
    return pl.pallas_call(
        attention_kernel,
        grid=(kv_local, group),
        out_shape=(
            jax.ShapeDtypeStruct((tokens, heads * HD), bf16),
            jax.ShapeDtypeStruct((tokens, heads * HD), bf16),
            jax.ShapeDtypeStruct((tokens, kv_local * HD), bf16),
            jax.ShapeDtypeStruct((tokens, kv_local * HD), bf16),
        ),
        in_specs=[
            pl.BlockSpec(memory_space=pltpu.SMEM),
            per_head,
            pl.BlockSpec((tokens, HD), lambda g, m: (0, heads + g)),
            pl.BlockSpec((tokens, HD), lambda g, m: (0, heads + kv_local + g)),
            cache,
            cache,
            per_head,
        ],
        out_specs=[per_head, per_head, per_kv, per_kv],
        scratch_shapes=[pltpu.VMEM((tokens, HD), jnp.float32)] * 2,
        compiler_params=pltpu.CompilerParams(vmem_limit_bytes=VMEM_LIMIT),
        name="attention",
    )(starts, proj, proj, proj, key_cache, value_cache, grad_out)


def head_work(heads, group, per_step, ins, outs, accs, hid_ref, full_ref, proj):
    bias_ref, kc_ref, vc_ref, go_ref = ins
    proj_ref, full_buf, full_sem = proj
    load = pltpu.make_async_copy(full_ref, full_buf, full_sem)
    load.start()
    att_ref, grads_ref = outs
    gk_acc, gv_acc = accs
    kvs = heads // group
    key_at, value_at = heads * HD, (heads + kvs) * HD
    factor = HD ** (-0.5)
    rows = proj_ref.shape[0]

    def one(head):
        g = head // group
        q_cols = pl.ds(pl.multiple_of(head * HD, HD), HD)
        kv_cols = pl.ds(pl.multiple_of(g * HD, HD), HD)
        q, go = proj_ref[:, q_cols], go_ref[:, q_cols]
        kn = proj_ref[:, pl.ds(pl.multiple_of(key_at + g * HD, HD), HD)]
        vn = proj_ref[:, pl.ds(pl.multiple_of(value_at + g * HD, HD), HD)]
        kc, vc = kc_ref[:, kv_cols], vc_ref[:, kv_cols]
        s_c = contract_last(q, kc) + bias_ref[...]
        row = lax.broadcasted_iota(jnp.int32, (rows, rows), 0)
        col = lax.broadcasted_iota(jnp.int32, (rows, rows), 1)
        s_o = jnp.where(col <= row, contract_last(q, kn), -jnp.inf)
        top = jnp.maximum(
            jnp.max(s_c, axis=-1, keepdims=True), jnp.max(s_o, axis=-1, keepdims=True)
        )
        e_c = jnp.exp2((s_c - top) * (factor * LOG2E))
        e_o = jnp.exp2((s_o - top) * (factor * LOG2E))
        total = jnp.sum(e_c, axis=-1, keepdims=True) + jnp.sum(e_o, axis=-1, keepdims=True)
        inverse = 1.0 / total
        p_c = (e_c * inverse).astype(jnp.bfloat16)
        p_o = (e_o * inverse).astype(jnp.bfloat16)
        att = jnp.dot(p_c, vc, preferred_element_type=jnp.float32) + jnp.dot(
            p_o, vn, preferred_element_type=jnp.float32
        )
        att_ref[:, q_cols] = att.astype(jnp.bfloat16)
        row_dot = jnp.sum(att * go.astype(jnp.float32), axis=-1, keepdims=True)
        g_c = contract_last(go, vc) - row_dot
        g_o = contract_last(go, vn) - row_dot
        ds_c = (p_c.astype(jnp.float32) * g_c * factor).astype(jnp.bfloat16)
        ds_o = (p_o.astype(jnp.float32) * g_o * factor).astype(jnp.bfloat16)
        gq = jnp.dot(ds_c, kc, preferred_element_type=jnp.float32) + jnp.dot(
            ds_o, kn, preferred_element_type=jnp.float32
        )
        grads_ref[:, q_cols] = gq.astype(jnp.bfloat16)
        gk_acc[g] += contract_first(ds_o, q)
        gv_acc[g] += contract_first(p_o, go)

    def project():
        load.wait()
        width = proj_ref.shape[1]
        tile = 384 if width % 384 == 0 else 128

        def each(t, carry):
            at = pl.ds(pl.multiple_of(t * tile, 128), tile)
            proj_ref[:, at] = jnp.dot(
                hid_ref[...], full_buf[:, at], preferred_element_type=jnp.float32
            ).astype(jnp.bfloat16)
            return carry

        lax.fori_loop(0, width // tile, each, 0)

    def work(step):
        @pl.when(step == 0)
        def _():
            project()

        @pl.when(step > 0)
        def _():
            def each(j, carry):
                head = (step - 1) * per_step + j

                @pl.when(head < heads)
                def _():
                    one(head)

                return carry

            lax.fori_loop(0, per_step, each, 0)

    def finish():
        for g in range(kvs):
            grads_ref[:, key_at + g * HD : key_at + (g + 1) * HD] = gk_acc[g].astype(jnp.bfloat16)
            grads_ref[:, value_at + g * HD : value_at + (g + 1) * HD] = gv_acc[g].astype(
                jnp.bfloat16
            )

    gk_acc[...] = jnp.zeros_like(gk_acc)
    gv_acc[...] = jnp.zeros_like(gv_acc)
    return work, finish


def gather_attend_kernel(
    n, heads, group, w_ref, prev_ref, hid_ref, bias_ref, kc_ref, vc_ref, go_ref,
    full_ref, att_ref, grads_ref, gk_acc, gv_acc, proj, full_buf, full_sem, *sems,
):
    work, finish = head_work(
        heads, group, -(-heads // (n - 2)), (bias_ref, kc_ref, vc_ref, go_ref),
        (att_ref, grads_ref), (gk_acc, gv_acc), hid_ref, prev_ref, (proj, full_buf, full_sem),
    )
    gather_ring(n, w_ref, full_ref, sems, None, work)
    finish()


def scatter_attend_kernel(
    n, heads, group, scale, hid_ref, mate_ref, done_ref, full_ref, bias_ref, kc_ref, vc_ref,
    go_ref, out_ref, att_ref, grads_ref, gk_acc, gv_acc, proj, full_buf, full_sem, *scratch,
):
    work, finish = head_work(
        heads, group, -(-heads // (n - 2)), (bias_ref, kc_ref, vc_ref, go_ref),
        (att_ref, grads_ref), (gk_acc, gv_acc), hid_ref, full_ref, (proj, full_buf, full_sem),
    )
    scatter_ring(n, 1, scale, hid_ref, mate_ref, done_ref, out_ref, scratch, None, work)
    finish()


def scatter_input_kernel(
    n, scale, hid_ref, mate_ref, first_ref, second_ref, wa_ref, wb_ref, out_ref, gin_ref,
    wa_buf, wb_buf, own, term, mate_term, wa_sem, wb_sem, term_send, term_recv, *scratch,
):
    tp_me = lax.axis_index("tp")
    span = wa_buf.shape[1]
    steps = n // 2

    def load(c):
        first_row = ((tp_me + 1 + c // steps) % 2) * (steps * span) + (c % steps) * span
        at = pl.ds(pl.multiple_of(first_row, 128), span)
        slot = c % 2
        return (
            pltpu.make_async_copy(wa_ref.at[at], wa_buf.at[slot], wa_sem.at[slot]),
            pltpu.make_async_copy(wb_ref.at[at], wb_buf.at[slot], wb_sem.at[slot]),
        )

    def send():
        return pltpu.make_async_remote_copy(
            src_ref=term, dst_ref=mate_term, send_sem=term_send, recv_sem=term_recv,
            device_id={"tp": (tp_me + 1) % 2}, device_id_type=MESH,
        )

    def before():
        for copy in load(0):
            copy.start()

    def work(step):
        @pl.when(step < n - 1)
        def _():
            for copy in load(step + 1):
                copy.start()

        for copy in load(step):
            copy.wait()
        value = contract_last(first_ref[...], wa_buf[step % 2]) + contract_last(
            second_ref[...], wb_buf[step % 2]
        )
        at = pl.ds(pl.multiple_of((step % steps) * span, 128), span)

        @pl.when(step < steps)
        def _():
            term[:, at] = value.astype(jnp.bfloat16)

        @pl.when(step >= steps)
        def _():
            own[:, at] = value

        @pl.when(step == steps - 1)
        def _():
            send().start()

    scatter_ring(n, 2, scale, hid_ref, mate_ref, second_ref, out_ref, scratch, before, work)
    send().wait()
    gin_ref[...] = (own[...] + mate_term[...].astype(jnp.float32)).astype(jnp.bfloat16)


def in_phases(blk_count, hidden, w_query, w_key, w_value, starts, key_cache, value_cache, grad_out):
    n = blk_count // 2
    tokens, depth = hidden.shape
    height, cached, group = depth // blk_count, key_cache.shape[1], H // KV
    kvs = w_key.shape[1] // HD // 2
    heads = kvs * group
    q_cols, kv_cols = heads * HD, kvs * HD
    width = q_cols + 2 * kv_cols
    scale = (tokens * blk_count) ** (-0.5)
    f32, bf16 = jnp.float32, jnp.bfloat16
    dma = pltpu.SemaphoreType.DMA
    vmem = pl.BlockSpec(memory_space=pltpu.VMEM)
    hbm = pl.BlockSpec(memory_space=pl.ANY)
    shape = jax.ShapeDtypeStruct

    def cut(i):
        kv = slice(i * kv_cols, (i + 1) * kv_cols)
        qs = slice(i * q_cols, (i + 1) * q_cols)
        w = jnp.concatenate([w_query[:, qs], w_key[:, kv], w_value[:, kv]], 1)
        return w, key_cache[0, :, kv], value_cache[0, :, kv], grad_out[:, qs]

    def params(number):
        return pltpu.CompilerParams(
            collective_id=number, has_side_effects=True, vmem_limit_bytes=VMEM_LIMIT
        )

    slots = lax.broadcasted_iota(jnp.int32, (1, cached), 1)
    bias = jnp.where(slots < starts[0], 0.0, -jnp.inf).astype(f32)
    accs = [pltpu.VMEM((kvs, tokens, HD), f32)] * 2
    accs += [pltpu.VMEM((tokens, width), bf16), pltpu.VMEM((depth, width), bf16), dma]
    w_a, kc_a, vc_a, go_a = cut(0)
    w_b, kc_b, vc_b, go_b = cut(1)
    full_a, mate = gather(w_a, hidden, blk_count)
    full_a = full_a.reshape(depth, width)
    full_b, att_a, grads_a = pl.pallas_call(
        functools.partial(gather_attend_kernel, n, heads, group),
        out_shape=(
            shape((blk_count, height, width), bf16),
            shape((tokens, q_cols), bf16),
            shape((tokens, width), bf16),
        ),
        in_specs=[hbm] * 2 + [vmem] * 5,
        out_specs=[hbm, vmem, vmem],
        scratch_shapes=accs + gather_sems(n),
        compiler_params=params(1),
        name="gather_attend",
    )(w_b, full_a, hidden, bias, kc_a, vc_a, go_a)
    full_b = full_b.reshape(depth, width)
    sum_a, att_b, grads_b = pl.pallas_call(
        functools.partial(scatter_attend_kernel, n, heads, group, scale),
        out_shape=(
            shape((height, width), f32),
            shape((tokens, q_cols), bf16),
            shape((tokens, width), bf16),
        ),
        in_specs=[vmem] * 3 + [hbm] + [vmem] * 4,
        out_specs=[vmem] * 3,
        scratch_shapes=accs + scatter_scratch(n, tokens, height, width),
        compiler_params=params(2),
        name="scatter_attend",
    )(hidden, mate, grads_a, full_b, bias, kc_b, vc_b, go_b)
    sum_b, grad_in = pl.pallas_call(
        functools.partial(scatter_input_kernel, n, scale),
        out_shape=(shape((height, width), f32), shape((tokens, depth // 2), bf16)),
        in_specs=[vmem] * 4 + [hbm] * 2,
        out_specs=[vmem] * 2,
        scratch_shapes=[
            pltpu.VMEM((2, depth // n, width), bf16),
            pltpu.VMEM((2, depth // n, width), bf16),
            pltpu.VMEM((tokens, depth // 2), f32),
            pltpu.VMEM((tokens, depth // 2), bf16),
            pltpu.VMEM((tokens, depth // 2), bf16),
            dma((2,)),
            dma((2,)),
            dma,
            dma,
        ]
        + scatter_scratch(n, tokens, height, width),
        compiler_params=params(3),
        name="scatter_input",
    )(hidden, mate, grads_a, grads_b, full_a, full_b)

    def join(first, last):
        return jnp.concatenate([sum_a[:, first:last], sum_b[:, first:last]], 1)

    return (
        jnp.concatenate([att_a, att_b], 1),
        grad_in,
        join(0, q_cols),
        join(q_cols, q_cols + kv_cols),
        join(q_cols + kv_cols, width),
    )


def local(blk_count, tp_count, hidden_in, w_query, w_key, w_value, starts, key_cache, value_cache, grad_out):
    tokens_dev, depth = hidden_in.shape
    if tp_count == 2 and (w_key.shape[1] // HD) % 2 == 0 and blk_count % 4 == 0:
        return in_phases(
            blk_count, hidden_in, w_query, w_key, w_value, starts, key_cache, value_cache, grad_out
        )
    w = jnp.concatenate([w_query, w_key, w_value], 1)
    full, mate = gather(w, hidden_in, blk_count)
    full = full.reshape(depth, w.shape[1])
    proj = jnp.dot(hidden_in, full, preferred_element_type=jnp.float32).astype(jnp.bfloat16)
    attended, grad_query, grad_keys, grad_values = attention(
        starts, proj, key_cache, value_cache, grad_out
    )
    grads = jnp.concatenate([grad_query, grad_keys, grad_values], 1)
    term = contract_last(grads, full)
    scale = (tokens_dev * blk_count) ** (-0.5)
    summed, others = scatter(
        hidden_in, mate, grads, term.astype(jnp.bfloat16), blk_count, tp_count, scale
    )
    width = depth // tp_count
    grad_in = lax.dynamic_slice_in_dim(term, lax.axis_index("tp") * width, width, 1)
    for k in range(tp_count - 1):
        grad_in = grad_in + others[k].astype(jnp.float32)
    grad_in = grad_in.astype(jnp.bfloat16)
    query_cols, kv_cols = w_query.shape[1], w_key.shape[1]
    return (
        attended,
        grad_in,
        summed[:, :query_cols],
        summed[:, query_cols : query_cols + kv_cols],
        summed[:, query_cols + kv_cols :],
    )


def solution(mesh):
    in_specs = (
        P("blk", None),
        P("blk", "tp"),
        P("blk", "tp"),
        P("blk", "tp"),
        P("blk"),
        P("blk", None, "tp"),
        P("blk", None, "tp"),
        P("blk", "tp"),
    )
    out_specs = (P("blk", "tp"),) * 5
    return jax.shard_map(
        functools.partial(local, mesh.shape["blk"], mesh.shape["tp"]),
        mesh=mesh,
        in_specs=in_specs,
        out_specs=out_specs,
        check_vma=False,
    )
```
